32 devices in a mesh: groups: 2 (over x), row: 16 (over z, y, core).
Axes of the slice: x: 2, y: 2, z: 4, core: 2. Of those that a mesh axis runs over, the one named last changes fastest.
Arguments:
- normals: bfloat16 [128, 32768], P('groups', 'row'), parts along dimension 0, may hold values from -6 to 6
- variance: float32 [65536], P(('groups', 'row')), parts along dimension 0, may hold values from 0.3 to 3
- tiles: bfloat16 [640, 512, 512], P(('groups', 'row')), parts along dimension 0, may hold values from -0.078125 to 0.078125
- tile_ids: int32 [640, 2], P(('groups', 'row')), parts along dimension 0, may hold values from -1 to 63, as said below
Outputs:
- lanczos_basis: float32 [4, 128, 32768], P(None, 'groups', 'row'), parts along dimension 1
- alphas: float32 [3, 128], P(None, 'groups'), parts along dimension 1
- betas: float32 [3, 128], P(None, 'groups'), parts along dimension 1
The draws below stay inside these ranges and needn't reach their ends.
There are 2 independent parts, one for each index of `groups`. The reference program is written for one: setup_inputs(seed, part) draws one part's arguments, and reference() takes and returns one part's arrays. A program takes and returns all parts, laid end to end along the dimension named above; each array names one. Nothing has to cross between parts.
Inputs may be any that keep to these rules, and one draw needn't show every extreme that they name: `tile_ids`: on the device at index d of row, every used slot holds a tile row i among d * 4 .. d * 4 + 3 and a tile column j with i - 4 <= j <= i, j >= 0; each pair appears at most once in a part; every diagonal pair (i, i) appears; an unused slot holds -1 in both entries; in every draw some device uses all 20 slots.
All inputs are finite; a program needn't handle non-finite values.
Results may differ from the reference program's by a relative error of at most 0.0059.
Values may be sent and summed in bfloat16 or wider, within the bound.
A program may use at most 128 MiB of HBM per device.

```python
import math
import jax
import jax.numpy as jnp
from jax import lax

TILE = 512
TR_DEV = 4
VEC = 64
ITERS = 3
BAND = 5
SLOTS = 20
ORDER = 32768
N_ROW = 16


def draw_tile_ids(key, part):
    device = jnp.arange(N_ROW)[:, None, None]
    within = jnp.arange(TR_DEV)[None, :, None]
    offset = jnp.arange(BAND)[None, None, :]
    row_id = device * TR_DEV + within + offset * 0
    col_id = row_id - offset
    valid = col_id >= 0
    key_rate, key_roll, key_full, key_order = jax.random.split(key, 4)
    rate = jax.random.randint(key_rate, (N_ROW, 1, 1), 20, 101)
    roll = jax.random.randint(key_roll, (N_ROW, TR_DEV, BAND), 0, 100)
    full_dev = jax.random.randint(key_full, (), 1, N_ROW)
    keep = valid & ((offset == 0) | (roll < rate) | (device == full_dev))
    row_vals = jnp.where(keep, row_id, -1).reshape(N_ROW, SLOTS)
    col_vals = jnp.where(keep, col_id, -1).reshape(N_ROW, SLOTS)
    score = jax.random.randint(key_order, (N_ROW, SLOTS), 0, 1 << 20) * SLOTS + jnp.arange(SLOTS)[None, :]
    order_idx = jnp.argsort(score, axis=1)
    row_vals = jnp.take_along_axis(row_vals, order_idx, 1)
    col_vals = jnp.take_along_axis(col_vals, order_idx, 1)
    return jnp.stack([row_vals.reshape(-1), col_vals.reshape(-1)], axis=1).astype(jnp.int32)


def level_of(stream_key, dims, cuts, smallest, top_value):
    factor_of, own = 1.0, jax.random.fold_in(stream_key, 6)
    for axis_at, parts in cuts:
        heights = jnp.exp(jax.random.uniform(jax.random.fold_in(own, axis_at), (parts,), jnp.float32, smallest / len(cuts), top_value / len(cuts)))
        factor_of = factor_of * jnp.repeat(heights, dims[axis_at] // parts).reshape([-1 if axis == axis_at else 1 for axis in range(len(dims))])
    return factor_of


def scatter_about(own_key, shape, scale, most, pieces=(), dtype=jnp.bfloat16):
    values = scale * jax.random.normal(own_key, shape, jnp.float32)
    if pieces:
        values = values * level_of(own_key, shape, pieces, -0.22, 0.18)
    return jnp.clip(values, -most, most).astype(dtype)


def setup_inputs(seed: int = 0, part: int = 0) -> dict:
    key_of = jax.random.split(jax.random.key(seed), 5)
    own_keys = jax.random.split(jax.random.fold_in(key_of[4], part), 5)
    normals = scatter_about(own_keys[0], (VEC, ORDER), 1.0, 6.0, ((1, 16),))
    variance = jnp.clip(jnp.exp(math.log(3.0) - 2.3025851 * jax.random.uniform(own_keys[1], (ORDER,), jnp.float32) ** level_of(own_keys[1], (ORDER,), ((0, 16),), -0.2, 0.2)), 0.3, 3.0)
    tiles = scatter_about(own_keys[2], (SLOTS * N_ROW, TILE, TILE), (2 * BAND * TILE) ** -0.5, 0.078125, ((0, 16),))
    tile_ids = draw_tile_ids(jax.random.fold_in(jax.random.fold_in(key_of[4], part), 71), part)
    return {"normals": normals, "variance": variance, "tiles": tiles, "tile_ids": tile_ids}


def apply_tiles(vq, tiles, tile_ids):

    def add_tile(totals, entries):
        tile_val, slot_ids = entries
        is_live = (slot_ids[0] >= 0).astype(jnp.float32)
        row_block = jnp.maximum(slot_ids[0], 0).astype(jnp.int32) * TILE
        col_block = jnp.maximum(slot_ids[1], 0).astype(jnp.int32) * TILE
        piece_col = lax.dynamic_slice_in_dim(vq, col_block, TILE, 1)
        piece_row = lax.dynamic_slice_in_dim(vq, row_block, TILE, 1)
        forward = jnp.dot(piece_col, tile_val.T, preferred_element_type=jnp.float32) * is_live
        backward = jnp.dot(piece_row, tile_val, preferred_element_type=jnp.float32) * is_live
        old_rows = lax.dynamic_slice_in_dim(totals, row_block, TILE, 1)
        totals = lax.dynamic_update_slice_in_dim(totals, old_rows + forward, row_block, 1)
        old_cols = lax.dynamic_slice_in_dim(totals, col_block, TILE, 1)
        totals = lax.dynamic_update_slice_in_dim(totals, old_cols + backward, col_block, 1)
        return (totals, None)
    start = jnp.zeros((VEC, ORDER), jnp.float32)
    totals, unused = lax.scan(add_tile, start, (tiles, tile_ids))
    return totals

def reference(normals, variance, tiles, tile_ids):
    draws_f = normals.astype(jnp.float32)
    norm_start = jnp.sqrt(lax.optimization_barrier(jnp.sum(draws_f * draws_f, axis=1)))
    vector = draws_f / norm_start[:, None]
    basis = [vector]
    alpha_list = []
    beta_list = []
    for levels in range(ITERS):
        vq = vector.astype(jnp.bfloat16)
        image_vec = variance[None, :] * vector + apply_tiles(vq, tiles, tile_ids)
        stacked = jnp.stack(basis)
        proj = lax.optimization_barrier(jnp.sum(stacked * image_vec[None], axis=2))
        image_vec = image_vec - lax.optimization_barrier(jnp.sum(stacked * proj[:, :, None], axis=0))
        beta_now = jnp.sqrt(lax.optimization_barrier(jnp.sum(image_vec * image_vec, axis=1)) + 1e-06)
        vector = image_vec / beta_now[:, None]
        alpha_list.append(proj[levels])
        beta_list.append(beta_now)
        basis.append(vector)
    return (jnp.stack(basis) * math.sqrt(ORDER), jnp.stack(alpha_list), jnp.stack(beta_list))
```

```python
import functools
import math

import jax
import jax.numpy as jnp
from jax import lax
from jax.experimental import pallas as pl
from jax.experimental.pallas import tpu as pltpu
from jax.sharding import PartitionSpec as P

ITERS = 3
EPS = 1e-06
LANES = 128


def dot(a, b, transposed):
    dims = (((1,), (1 if transposed else 0,)), ((), ()))
    return lax.dot_general(a, b, dims, preferred_element_type=jnp.float32)


def lane_sums(value):
    total = value[:, :LANES]
    for at in range(LANES, value.shape[1], LANES):
        total = total + value[:, at : at + LANES]
    return total


def as_row(first, second):
    stacked = jnp.concatenate([first, second], axis=0)
    return jnp.sum(jnp.transpose(stacked), axis=0, keepdims=True)


def as_columns(row):
    return jnp.transpose(jnp.broadcast_to(row, (LANES, LANES)))


def kernel(
    n, ids, normals, variance, tiles, basis_out, alphas, betas,
    tiles_v, vq, prev, reach_s, reach_r, basis, image, psend, precv, slot_map, live_map,
    tile_sem, halo_send, halo_recv, back_send, back_recv, msg_send, msg_recv, out_sem,
):
    me = lax.axis_index("row")
    slots, width, _ = tiles.shape
    vecs, sites = normals.shape
    blocks = sites // width
    band = blocks + 1

    def tile_copy(s):
        return pltpu.make_async_copy(tiles.at[s], tiles_v.at[s], tile_sem.at[s])

    for s in range(slots):
        tile_copy(s).start()

    barrier = pltpu.get_barrier_semaphore()

    def greet(o, carry):
        pl.semaphore_signal(
            barrier, inc=1, device_id={"row": lax.rem(me + o, n)}, device_id_type=pl.DeviceIdType.MESH
        )
        return carry

    lax.fori_loop(1, n, greet, 0)

    def block(at):
        return pl.ds(at * width, width)

    def wide(column):
        return jnp.concatenate([column] * (width // LANES), axis=1)

    def halo_copy(k):
        return pltpu.make_async_remote_copy(
            src_ref=vq.at[k], dst_ref=prev.at[k], send_sem=halo_send.at[k], recv_sem=halo_recv.at[k],
            device_id={"row": lax.rem(me + 1, n)}, device_id_type=pl.DeviceIdType.MESH,
        )

    def back_copy(k):
        return pltpu.make_async_remote_copy(
            src_ref=reach_s.at[k], dst_ref=reach_r.at[k], send_sem=back_send.at[k], recv_sem=back_recv.at[k],
            device_id={"row": lax.rem(me + n - 1, n)}, device_id_type=pl.DeviceIdType.MESH,
        )

    def send_message(e, message):
        psend[e] = message
        precv[e, me] = message

        def send(o, carry):
            pltpu.make_async_remote_copy(
                src_ref=psend.at[e], dst_ref=precv.at[e, me], send_sem=msg_send.at[e], recv_sem=msg_recv.at[e],
                device_id={"row": lax.rem(me + o, n)}, device_id_type=pl.DeviceIdType.MESH,
            ).start()
            return carry

        lax.fori_loop(1, n, send, 0)

    def total_message(e):
        everyone = precv.at[e, pl.ds(0, n - 1)]
        pltpu.make_async_copy(everyone, everyone, msg_recv.at[e]).wait()
        return jnp.sum(precv[e], axis=0)

    def finish_message(e):
        everyone = precv.at[e, pl.ds(0, n - 1)]
        pltpu.make_async_copy(everyone, everyone, msg_send.at[e]).wait()

    def message(*rows):
        pad = jnp.zeros((8 - len(rows), LANES), jnp.float32)
        return jnp.concatenate([*rows, pad], axis=0)

    squares = jnp.zeros((vecs, LANES), jnp.float32)
    for j in range(blocks):
        raw = normals[:, block(j)]
        vq[0, :, block(j)] = raw
        value = raw.astype(jnp.float32)
        basis[0, :, block(j)] = value
        squares = squares + lane_sums(value * value)
        for m in range(1, ITERS):
            basis[m, :, block(j)] = jnp.zeros_like(value)
    start_message = message(as_row(squares, squares))

    @pl.when(me == 0)
    def _():
        prev[...] = jnp.zeros_like(prev)

    @pl.when(me == n - 1)
    def _():
        reach_r[...] = jnp.zeros_like(reach_r)

    pl.semaphore_wait(barrier, n - 1)
    send_message(ITERS, start_message)

    @pl.when(me < n - 1)
    def _():
        halo_copy(0).start()

    codes = [(ids[s, 0] - me * blocks) * band + (ids[s, 0] - ids[s, 1]) for s in range(slots)]

    def locate(p, carry):
        slot, live = jnp.int32(0), jnp.float32(0)
        for s, code in enumerate(codes):
            slot = jnp.where(code == p, jnp.int32(s), slot)
            live = jnp.where(code == p, jnp.float32(1), live)
        slot_map[p] = slot
        live_map[p] = live
        return carry

    lax.fori_loop(0, blocks * band, locate, 0)

    def product(left, i, offset, transposed):
        p = i * band + offset
        return dot(left, tiles_v[slot_map[p]], transposed) * live_map[p]

    for s in range(slots):
        tile_copy(s).wait()

    def normalise(k, eps):
        row = jnp.sqrt(total_message(ITERS + k)[0:1] + eps)
        inverse = wide(1.0 / as_columns(row)[:vecs])
        for j in range(blocks):
            basis[k, :, block(j)] = basis[k, :, block(j)] * inverse
        pltpu.make_async_copy(basis.at[k], basis_out.at[k], out_sem.at[k]).start()
        return row, inverse

    def step(k, carry):
        for c in range(blocks):
            total = None
            for i in range(c + 1):
                term = product(vq[k, :, block(i)], i, i + blocks - c, False)
                total = term if total is None else total + term
            reach_s[k, :, block(c)] = total.astype(jnp.bfloat16)

        @pl.when(me > 0)
        def _():
            back_copy(k).start()

        for j in range(blocks):
            total = None
            for i in range(j, blocks):
                term = product(vq[k, :, block(i)], i, i - j, False)
                total = term if total is None else total + term
            for c in range(j + 1):
                total = total + product(vq[k, :, block(c)], j, j - c, True)
            image[:, block(j)] = total

        row, inverse = normalise(k, jnp.where(k == 0, 0.0, EPS))

        @pl.when(k > 0)
        def _():
            betas[pl.ds(jnp.maximum(k - 1, 0), 1), :] = row[:, :vecs]

        @pl.when(me > 0)
        def _():
            halo_copy(k).wait_recv()

        for j in range(blocks):
            total = image[:, block(j)]
            for c in range(j, blocks):
                total = total + product(prev[k, :, block(c)], j, j + blocks - c, True)
            image[:, block(j)] = total

        @pl.when(me < n - 1)
        def _():
            back_copy(k).wait_recv()

        parts = [jnp.zeros((vecs, LANES), jnp.float32) for _ in range(ITERS)]
        for j in range(blocks):
            value = (image[:, block(j)] + reach_r[k, :, block(j)].astype(jnp.float32)) * inverse
            value = value + variance[:, block(j)] * basis[k, :, block(j)]
            image[:, block(j)] = value
            for m in range(ITERS):
                parts[m] = parts[m] + lane_sums(basis[m, :, block(j)] * value)
        send_message(k, message(as_row(parts[0], parts[1]), as_row(parts[2], parts[2])))
        sums = total_message(k)
        low, high = as_columns(sums[0:1]), as_columns(sums[1:2])
        proj = [wide(low[:vecs]), wide(low[vecs : 2 * vecs]), wide(high[:vecs])]
        chosen = jnp.where(k == 0, sums[0:1, :vecs], jnp.where(k == 1, sums[0:1, vecs : 2 * vecs], sums[1:2, :vecs]))
        alphas[pl.ds(k, 1), :] = chosen
        squares = jnp.zeros((vecs, LANES), jnp.float32)
        for j in range(blocks):
            value = image[:, block(j)]
            lost = basis[0, :, block(j)] * proj[0]
            for m in range(1, ITERS):
                lost = lost + basis[m, :, block(j)] * proj[m]
            value = value - lost
            basis[k + 1, :, block(j)] = value
            vq[k + 1, :, block(j)] = value.astype(jnp.bfloat16)
            squares = squares + lane_sums(value * value)

        @pl.when((k < ITERS - 1) & (me < n - 1))
        def _():
            halo_copy(k + 1).start()

        send_message(ITERS + k + 1, message(as_row(squares, squares)))
        return carry

    lax.fori_loop(0, ITERS, step, 0)
    row, _ = normalise(ITERS, EPS)
    betas[ITERS - 1 : ITERS, :] = row[:, :vecs]

    for k in range(ITERS):
        @pl.when(me < n - 1)
        def _():
            halo_copy(k).wait_send()

        @pl.when(me > 0)
        def _():
            back_copy(k).wait_send()

    for e in range(2 * ITERS + 1):
        finish_message(e)
    for k in range(ITERS + 1):
        pltpu.make_async_copy(basis.at[k], basis_out.at[k], out_sem.at[k]).wait()


def shards(n, normals, variance, tiles, tile_ids):
    vecs, sites = normals.shape
    slots, width, _ = tiles.shape
    band = sites // width + 1
    places = band * (sites // width)
    messages = 2 * ITERS + 1
    vmem = pl.BlockSpec(memory_space=pltpu.VMEM)
    any_space = pl.BlockSpec(memory_space=pl.ANY)
    dma = pltpu.SemaphoreType.DMA
    basis, alphas, betas = pl.pallas_call(
        functools.partial(kernel, n),
        out_shape=(
            jax.ShapeDtypeStruct((ITERS + 1, vecs, sites), jnp.float32),
            jax.ShapeDtypeStruct((ITERS, vecs), jnp.float32),
            jax.ShapeDtypeStruct((ITERS, vecs), jnp.float32),
        ),
        in_specs=[pl.BlockSpec(memory_space=pltpu.SMEM), vmem, vmem, any_space],
        out_specs=(any_space, vmem, vmem),
        scratch_shapes=[
            pltpu.VMEM((slots, width, width), jnp.bfloat16),
            pltpu.VMEM((ITERS + 1, vecs, sites), jnp.bfloat16),
            pltpu.VMEM((ITERS, vecs, sites), jnp.bfloat16),
            pltpu.VMEM((ITERS, vecs, sites), jnp.bfloat16),
            pltpu.VMEM((ITERS, vecs, sites), jnp.bfloat16),
            pltpu.VMEM((ITERS + 1, vecs, sites), jnp.float32),
            pltpu.VMEM((vecs, sites), jnp.float32),
            pltpu.VMEM((messages, 8, LANES), jnp.float32),
            pltpu.VMEM((messages, n, 8, LANES), jnp.float32),
            pltpu.SMEM((places,), jnp.int32),
            pltpu.SMEM((places,), jnp.float32),
            dma((slots,)),
            dma((ITERS,)),
            dma((ITERS,)),
            dma((ITERS,)),
            dma((ITERS,)),
            dma((messages,)),
            dma((messages,)),
            dma((ITERS + 1,)),
        ],
        compiler_params=pltpu.CompilerParams(
            collective_id=0, has_side_effects=True, vmem_limit_bytes=48 * 1024 * 1024
        ),
    )(tile_ids, normals, variance[None, :], tiles)
    return basis * math.sqrt(sites * n), alphas, betas


def solution(mesh):
    return jax.shard_map(
        functools.partial(shards, mesh.shape["row"]),
        mesh=mesh,
        in_specs=(
            P("groups", "row"),
            P(("groups", "row")),
            P(("groups", "row"), None, None),
            P(("groups", "row"), None),
        ),
        out_specs=(P(None, "groups", "row"), P(None, "groups"), P(None, "groups")),
        check_vma=False,
    )
```

```python
import functools
import math

import jax
import jax.numpy as jnp
from jax import lax
from jax.experimental import pallas as pl
from jax.experimental.pallas import tpu as pltpu
from jax.sharding import PartitionSpec as P

ITERS = 3
EPS = 1e-06
LANES = 128


def dot(a, b, transposed):
    dims = (((1,), (1 if transposed else 0,)), ((), ()))
    return lax.dot_general(a, b, dims, preferred_element_type=jnp.float32)


def lane_sums(value):
    total = value[:, :LANES]
    for at in range(LANES, value.shape[1], LANES):
        total = total + value[:, at : at + LANES]
    return total


def as_row(first, second):
    stacked = jnp.concatenate([first, second], axis=0)
    return jnp.sum(jnp.transpose(stacked), axis=0, keepdims=True)


def as_columns(row):
    return jnp.transpose(jnp.broadcast_to(row, (LANES, LANES)))


def kernel(
    n, ids, normals, variance, tiles, basis_out, alphas, betas,
    tiles_v, vq, prev, reach_s, reach_r, basis, applied, image, coef, psend, precv, slot_map, live_map,
    tile_sem, halo_send, halo_recv, back_send, back_recv, msg_send, msg_recv, out_sem,
):
    me = lax.axis_index("row")
    slots, width, _ = tiles.shape
    vecs, sites = normals.shape
    blocks = sites // width
    band = blocks + 1

    def tile_copy(s):
        return pltpu.make_async_copy(tiles.at[s], tiles_v.at[s], tile_sem.at[s])

    for s in range(slots):
        tile_copy(s).start()

    barrier = pltpu.get_barrier_semaphore()

    def greet(o, carry):
        pl.semaphore_signal(
            barrier, inc=1, device_id={"row": lax.rem(me + o, n)}, device_id_type=pl.DeviceIdType.MESH
        )
        return carry

    lax.fori_loop(1, n, greet, 0)

    def block(at):
        return pl.ds(at * width, width)

    def wide(column):
        return jnp.concatenate([column] * (width // LANES), axis=1)

    def halo_copy(k):
        return pltpu.make_async_remote_copy(
            src_ref=vq.at[k], dst_ref=prev.at[k], send_sem=halo_send.at[k], recv_sem=halo_recv.at[k],
            device_id={"row": lax.rem(me + 1, n)}, device_id_type=pl.DeviceIdType.MESH,
        )

    def back_copy(k, c):
        return pltpu.make_async_remote_copy(
            src_ref=reach_s.at[k, c], dst_ref=reach_r.at[k, c],
            send_sem=back_send.at[k, c], recv_sem=back_recv.at[k, c],
            device_id={"row": lax.rem(me + n - 1, n)}, device_id_type=pl.DeviceIdType.MESH,
        )

    def send_message(e, message):
        psend[e] = message
        precv[e, me] = message

        def send(o, carry):
            pltpu.make_async_remote_copy(
                src_ref=psend.at[e], dst_ref=precv.at[e, me], send_sem=msg_send.at[e], recv_sem=msg_recv.at[e],
                device_id={"row": lax.rem(me + o, n)}, device_id_type=pl.DeviceIdType.MESH,
            ).start()
            return carry

        lax.fori_loop(1, n, send, 0)

    def total_message(e):
        everyone = precv.at[e, pl.ds(0, n - 1)]
        pltpu.make_async_copy(everyone, everyone, msg_recv.at[e]).wait()
        return jnp.sum(precv[e], axis=0)

    def finish_message(e):
        everyone = precv.at[e, pl.ds(0, n - 1)]
        pltpu.make_async_copy(everyone, everyone, msg_send.at[e]).wait()

    def message(*rows):
        pad = jnp.zeros((8 - len(rows), LANES), jnp.float32)
        return jnp.concatenate([*rows, pad], axis=0)

    for j in range(blocks):
        raw = normals[:, block(j)]
        vq[0, :, block(j)] = raw
        basis[0, :, block(j)] = raw.astype(jnp.float32)
    for m in range(1, ITERS):
        basis[m] = jnp.zeros(basis.shape[1:], jnp.float32)
    for m in range(ITERS):
        applied[m] = jnp.zeros(applied.shape[1:], jnp.float32)
        coef[m] = jnp.zeros(coef.shape[1:], jnp.float32)
    coef[ITERS] = jnp.ones(coef.shape[1:], jnp.float32)

    @pl.when(me == 0)
    def _():
        prev[...] = jnp.zeros_like(prev)

    @pl.when(me == n - 1)
    def _():
        reach_r[...] = jnp.zeros_like(reach_r)

    pl.semaphore_wait(barrier, n - 1)

    @pl.when(me < n - 1)
    def _():
        halo_copy(0).start()

    codes = [(ids[0, s] - me * blocks) * band + (ids[0, s] - ids[1, s]) for s in range(slots)]

    def locate(p, carry):
        slot, live = jnp.int32(0), jnp.float32(0)
        for s, code in enumerate(codes):
            slot = jnp.where(code == p, jnp.int32(s), slot)
            live = jnp.where(code == p, jnp.float32(1), live)
        slot_map[p] = slot
        live_map[p] = live
        return carry

    lax.fori_loop(0, blocks * band, locate, 0)

    def product(left, i, offset, transposed):
        p = i * band + offset
        return dot(left, tiles_v[slot_map[p]], transposed) * live_map[p]

    for s in range(slots):
        tile_copy(s).wait()

    def write_out(k):
        return pltpu.make_async_copy(basis.at[k], basis_out.at[k], out_sem.at[k])

    def finalise(k):
        sums = total_message(k)
        norm = jnp.sqrt(sums[2:3] + jnp.where(k == 0, 0.0, EPS))
        inverse = 1.0 / norm
        second = jnp.where(lax.broadcasted_iota(jnp.int32, (1, LANES), 1) >= vecs, 1, 0)
        near = sums[0:1] * inverse * jnp.where(second == k, inverse, 1.0)
        far = sums[1:2] * inverse * jnp.where(second + 2 == k, inverse, 1.0)
        low, high = as_columns(near), as_columns(far)
        columns = [low[:vecs], low[vecs : 2 * vecs], high[:vecs], as_columns(inverse)[:vecs]]
        for m, column in enumerate(columns):
            coef[m] = column
        alphas[pl.ds(k, 1), :] = jnp.where(
            k == 0, near[:, :vecs], jnp.where(k == 1, near[:, vecs : 2 * vecs], far[:, :vecs])
        )

        @pl.when(k > 0)
        def _():
            betas[pl.ds((k + ITERS - 1) % ITERS, 1), :] = norm[:, :vecs]

        proj = [wide(column) for column in columns]
        squares = jnp.zeros((vecs, LANES), jnp.float32)
        for j in range(blocks):
            vector = basis[k, :, block(j)] * proj[ITERS]
            basis[k, :, block(j)] = vector
            product_part = applied[k, :, block(j)] * proj[ITERS]
            applied[k, :, block(j)] = product_part
            lost = basis[0, :, block(j)] * proj[0]
            for m in range(1, ITERS):
                lost = lost + basis[m, :, block(j)] * proj[m]
            value = variance[:, block(j)] * vector + product_part - lost
            basis[k + 1, :, block(j)] = value
            squares = squares + lane_sums(value * value)
        write_out(k).start()
        return squares

    def step(k, carry):
        for c in range(blocks):
            total = None
            for i in range(c + 1):
                term = product(vq[k, :, block(i)], i, i + blocks - c, False)
                total = term if total is None else total + term
            reach_s[k, c] = total.astype(jnp.bfloat16)

            @pl.when(me > 0)
            def _():
                back_copy(k, c).start()

        for j in range(blocks):
            total = None
            for i in range(j, blocks):
                term = product(vq[k, :, block(i)], i, i - j, False)
                total = term if total is None else total + term
            for c in range(j + 1):
                total = total + product(vq[k, :, block(c)], j, j - c, True)
            image[:, block(j)] = total

        @pl.when(k > 0)
        def _():
            finalise(jnp.maximum(k - 1, 0))

        @pl.when(me > 0)
        def _():
            halo_copy(k).wait_recv()

        for j in range(blocks):
            total = image[:, block(j)]
            for c in range(j, blocks):
                total = total + product(prev[k, :, block(c)], j, j + blocks - c, True)
            image[:, block(j)] = total

        parts = [jnp.zeros((vecs, LANES), jnp.float32) for _ in range(ITERS + 1)]
        proj = [wide(coef[m]) for m in range(ITERS + 1)]
        for j in range(blocks):
            @pl.when(me < n - 1)
            def _():
                back_copy(k, j).wait_recv()

            value = (image[:, block(j)] + reach_r[k, j].astype(jnp.float32)) * proj[ITERS]
            for m in range(ITERS):
                value = value - applied[m, :, block(j)] * proj[m]
            applied[k, :, block(j)] = value
            vector = basis[k, :, block(j)]
            value = value + variance[:, block(j)] * vector
            vq[k + 1, :, block(j)] = value.astype(jnp.bfloat16)
            for m in range(ITERS):
                parts[m] = parts[m] + lane_sums(basis[m, :, block(j)] * value)
            parts[ITERS] = parts[ITERS] + lane_sums(vector * vector)
        last = parts[ITERS]
        send_message(k, message(as_row(parts[0], parts[1]), as_row(parts[2], last), as_row(last, last)))

        @pl.when((k < ITERS - 1) & (me < n - 1))
        def _():
            halo_copy(k + 1).start()

        return carry

    lax.fori_loop(0, ITERS, step, 0)
    squares = finalise(ITERS - 1)
    send_message(ITERS, message(as_row(squares, squares)))
    row = jnp.sqrt(total_message(ITERS)[0:1] + EPS)
    betas[ITERS - 1 : ITERS, :] = row[:, :vecs]
    inverse = wide(1.0 / as_columns(row)[:vecs])
    for j in range(blocks):
        basis[ITERS, :, block(j)] = basis[ITERS, :, block(j)] * inverse
    write_out(ITERS).start()

    for k in range(ITERS):
        @pl.when(me < n - 1)
        def _():
            halo_copy(k).wait_send()

        @pl.when(me > 0)
        def _():
            for c in range(blocks):
                back_copy(k, c).wait_send()

    for e in range(ITERS + 1):
        finish_message(e)
    for k in range(ITERS + 1):
        write_out(k).wait()


def shards(n, normals, variance, tiles, tile_ids):
    vecs, sites = normals.shape
    slots, width, _ = tiles.shape
    band = sites // width + 1
    places = band * (sites // width)
    messages = ITERS + 1
    vmem = pl.BlockSpec(memory_space=pltpu.VMEM)
    any_space = pl.BlockSpec(memory_space=pl.ANY)
    dma = pltpu.SemaphoreType.DMA
    basis, alphas, betas = pl.pallas_call(
        functools.partial(kernel, n),
        out_shape=(
            jax.ShapeDtypeStruct((ITERS + 1, vecs, sites), jnp.float32),
            jax.ShapeDtypeStruct((ITERS, vecs), jnp.float32),
            jax.ShapeDtypeStruct((ITERS, vecs), jnp.float32),
        ),
        in_specs=[pl.BlockSpec(memory_space=pltpu.SMEM), vmem, vmem, any_space],
        out_specs=(any_space, vmem, vmem),
        scratch_shapes=[
            pltpu.VMEM((slots, width, width), jnp.bfloat16),
            pltpu.VMEM((ITERS + 1, vecs, sites), jnp.bfloat16),
            pltpu.VMEM((ITERS, vecs, sites), jnp.bfloat16),
            pltpu.VMEM((ITERS, sites // width, vecs, width), jnp.bfloat16),
            pltpu.VMEM((ITERS, sites // width, vecs, width), jnp.bfloat16),
            pltpu.VMEM((ITERS + 1, vecs, sites), jnp.float32),
            pltpu.VMEM((ITERS, vecs, sites), jnp.float32),
            pltpu.VMEM((vecs, sites), jnp.float32),
            pltpu.VMEM((ITERS + 1, vecs, LANES), jnp.float32),
            pltpu.VMEM((messages, 8, LANES), jnp.float32),
            pltpu.VMEM((messages, n, 8, LANES), jnp.float32),
            pltpu.SMEM((places,), jnp.int32),
            pltpu.SMEM((places,), jnp.float32),
            dma((slots,)),
            dma((ITERS,)),
            dma((ITERS,)),
            dma((ITERS, sites // width)),
            dma((ITERS, sites // width)),
            dma((messages,)),
            dma((messages,)),
            dma((ITERS + 1,)),
        ],
        compiler_params=pltpu.CompilerParams(
            collective_id=0, has_side_effects=True, vmem_limit_bytes=48 * 1024 * 1024
        ),
    )(tile_ids.T, normals, variance[None, :], tiles)
    return basis * math.sqrt(sites * n), alphas, betas


def solution(mesh):
    return jax.shard_map(
        functools.partial(shards, mesh.shape["row"]),
        mesh=mesh,
        in_specs=(
            P("groups", "row"),
            P(("groups", "row")),
            P(("groups", "row"), None, None),
            P(("groups", "row"), None),
        ),
        out_specs=(P(None, "groups", "row"), P(None, "groups"), P(None, "groups")),
        check_vma=False,
    )
```

```python
import functools
import math

import jax
import jax.numpy as jnp
from jax import lax
from jax.experimental import pallas as pl
from jax.experimental.pallas import tpu as pltpu
from jax.sharding import PartitionSpec as P

ITERS = 3
EPS = 1e-06
LANES = 128


def dot(a, b, transposed):
    dims = (((1,), (1 if transposed else 0,)), ((), ()))
    return lax.dot_general(a, b, dims, preferred_element_type=jnp.float32)


def lane_sums(value):
    total = value[:, :LANES]
    for at in range(LANES, value.shape[1], LANES):
        total = total + value[:, at : at + LANES]
    return total


def as_row(first, second):
    stacked = jnp.concatenate([first, second], axis=0)
    return jnp.sum(jnp.transpose(stacked), axis=0, keepdims=True)


def as_columns(row):
    return jnp.transpose(jnp.broadcast_to(row, (LANES, LANES)))


def kernel(
    n, ids, normals_in, variance_in, tiles, basis_out, alphas, betas,
    normals, variance, tiles_v, vq, prev, reach_s, reach_r, basis, applied, image, coef, psend, precv, slot_map, live_map,
    tile_sem, halo_send, halo_recv, back_send, back_recv, msg_send, msg_recv, out_sem, in_sem,
):
    me = lax.axis_index("row")
    slots, width, _ = tiles.shape
    vecs, sites = normals_in.shape
    blocks = sites // width
    band = blocks + 1

    def tile_copy(s):
        return pltpu.make_async_copy(tiles.at[s], tiles_v.at[s], tile_sem.at[s])

    draws_copy = pltpu.make_async_copy(normals_in, normals, in_sem.at[0])
    variance_copy = pltpu.make_async_copy(variance_in, variance, in_sem.at[1])
    draws_copy.start()
    variance_copy.start()
    for s in range(slots):
        tile_copy(s).start()

    barrier = pltpu.get_barrier_semaphore()

    def greet(o, carry):
        pl.semaphore_signal(
            barrier, inc=1, device_id={"row": lax.rem(me + o, n)}, device_id_type=pl.DeviceIdType.MESH
        )
        return carry

    lax.fori_loop(1, n, greet, 0)

    def block(at):
        return pl.ds(at * width, width)

    def wide(column):
        return jnp.concatenate([column] * (width // LANES), axis=1)

    def halo_copy(k):
        return pltpu.make_async_remote_copy(
            src_ref=vq.at[k], dst_ref=prev.at[k], send_sem=halo_send.at[k], recv_sem=halo_recv.at[k],
            device_id={"row": lax.rem(me + 1, n)}, device_id_type=pl.DeviceIdType.MESH,
        )

    def back_copy(k, c):
        return pltpu.make_async_remote_copy(
            src_ref=reach_s.at[k, c], dst_ref=reach_r.at[k, c],
            send_sem=back_send.at[k, c], recv_sem=back_recv.at[k, c],
            device_id={"row": lax.rem(me + n - 1, n)}, device_id_type=pl.DeviceIdType.MESH,
        )

    def send_message(e, message):
        psend[e] = message
        precv[e, me] = message

        def send(o, carry):
            pltpu.make_async_remote_copy(
                src_ref=psend.at[e], dst_ref=precv.at[e, me], send_sem=msg_send.at[e], recv_sem=msg_recv.at[e],
                device_id={"row": lax.rem(me + o, n)}, device_id_type=pl.DeviceIdType.MESH,
            ).start()
            return carry

        lax.fori_loop(1, n, send, 0)

    def total_message(e):
        everyone = precv.at[e, pl.ds(0, n - 1)]
        pltpu.make_async_copy(everyone, everyone, msg_recv.at[e]).wait()
        return jnp.sum(precv[e], axis=0)

    def finish_message(e):
        everyone = precv.at[e, pl.ds(0, n - 1)]
        pltpu.make_async_copy(everyone, everyone, msg_send.at[e]).wait()

    def message(*rows):
        pad = jnp.zeros((8 - len(rows), LANES), jnp.float32)
        return jnp.concatenate([*rows, pad], axis=0)

    draws_copy.wait()
    variance_copy.wait()

    for j in range(blocks):
        raw = normals[:, block(j)]
        vq[0, :, block(j)] = raw
        basis[0, :, block(j)] = raw.astype(jnp.float32)
    for m in range(1, ITERS):
        basis[m] = jnp.zeros(basis.shape[1:], jnp.float32)
    for m in range(ITERS):
        applied[m] = jnp.zeros(applied.shape[1:], jnp.float32)
        coef[m] = jnp.zeros(coef.shape[1:], jnp.float32)
    coef[ITERS] = jnp.ones(coef.shape[1:], jnp.float32)

    @pl.when(me == 0)
    def _():
        prev[...] = jnp.zeros_like(prev)

    @pl.when(me == n - 1)
    def _():
        reach_r[...] = jnp.zeros_like(reach_r)

    pl.semaphore_wait(barrier, n - 1)

    @pl.when(me < n - 1)
    def _():
        halo_copy(0).start()

    codes = [(ids[0, s] - me * blocks) * band + (ids[0, s] - ids[1, s]) for s in range(slots)]

    def locate(p, carry):
        slot, live = jnp.int32(0), jnp.float32(0)
        for s, code in enumerate(codes):
            slot = jnp.where(code == p, jnp.int32(s), slot)
            live = jnp.where(code == p, jnp.float32(1), live)
        slot_map[p] = slot
        live_map[p] = live
        return carry

    lax.fori_loop(0, blocks * band, locate, 0)

    def product(left, i, offset, transposed):
        p = i * band + offset
        return dot(left, tiles_v[slot_map[p]], transposed) * live_map[p]

    for s in range(slots):
        tile_copy(s).wait()

    def write_out(k):
        return pltpu.make_async_copy(basis.at[k], basis_out.at[k], out_sem.at[k])

    def finalise(k):
        sums = total_message(k)
        norm = jnp.sqrt(sums[2:3] + jnp.where(k == 0, 0.0, EPS))
        inverse = 1.0 / norm
        second = jnp.where(lax.broadcasted_iota(jnp.int32, (1, LANES), 1) >= vecs, 1, 0)
        near = sums[0:1] * inverse * jnp.where(second == k, inverse, 1.0)
        far = sums[1:2] * inverse * jnp.where(second + 2 == k, inverse, 1.0)
        low, high = as_columns(near), as_columns(far)
        columns = [low[:vecs], low[vecs : 2 * vecs], high[:vecs], as_columns(inverse)[:vecs]]
        for m, column in enumerate(columns):
            coef[m] = column
        alphas[pl.ds(k, 1), :] = jnp.where(
            k == 0, near[:, :vecs], jnp.where(k == 1, near[:, vecs : 2 * vecs], far[:, :vecs])
        )

        @pl.when(k > 0)
        def _():
            betas[pl.ds((k + ITERS - 1) % ITERS, 1), :] = norm[:, :vecs]

        proj = [wide(column) for column in columns]
        squares = jnp.zeros((vecs, LANES), jnp.float32)
        for j in range(blocks):
            vector = basis[k, :, block(j)] * proj[ITERS]
            basis[k, :, block(j)] = vector
            product_part = applied[k, :, block(j)] * proj[ITERS]
            applied[k, :, block(j)] = product_part
            lost = basis[0, :, block(j)] * proj[0]
            for m in range(1, ITERS):
                lost = lost + basis[m, :, block(j)] * proj[m]
            value = variance[:, block(j)] * vector + product_part - lost
            basis[k + 1, :, block(j)] = value
            squares = squares + lane_sums(value * value)
        write_out(k).start()
        return squares

    def step(k, carry):
        for c in range(blocks):
            total = None
            for i in range(c + 1):
                term = product(vq[k, :, block(i)], i, i + blocks - c, False)
                total = term if total is None else total + term
            reach_s[k, c] = total.astype(jnp.bfloat16)

            @pl.when(me > 0)
            def _():
                back_copy(k, c).start()

        for j in range(blocks):
            total = None
            for i in range(j, blocks):
                term = product(vq[k, :, block(i)], i, i - j, False)
                total = term if total is None else total + term
            for c in range(j + 1):
                total = total + product(vq[k, :, block(c)], j, j - c, True)
            image[:, block(j)] = total

        @pl.when(k > 0)
        def _():
            finalise(jnp.maximum(k - 1, 0))

        @pl.when(me > 0)
        def _():
            halo_copy(k).wait_recv()

        for j in range(blocks):
            total = image[:, block(j)]
            for c in range(j, blocks):
                total = total + product(prev[k, :, block(c)], j, j + blocks - c, True)
            image[:, block(j)] = total

        parts = [jnp.zeros((vecs, LANES), jnp.float32) for _ in range(ITERS + 1)]
        proj = [wide(coef[m]) for m in range(ITERS + 1)]
        for j in range(blocks):
            @pl.when(me < n - 1)
            def _():
                back_copy(k, j).wait_recv()

            value = (image[:, block(j)] + reach_r[k, j].astype(jnp.float32)) * proj[ITERS]
            for m in range(ITERS):
                value = value - applied[m, :, block(j)] * proj[m]
            applied[k, :, block(j)] = value
            vector = basis[k, :, block(j)]
            value = value + variance[:, block(j)] * vector
            vq[k + 1, :, block(j)] = value.astype(jnp.bfloat16)
            for m in range(ITERS):
                parts[m] = parts[m] + lane_sums(basis[m, :, block(j)] * value)
            parts[ITERS] = parts[ITERS] + lane_sums(vector * vector)
        last = parts[ITERS]
        send_message(k, message(as_row(parts[0], parts[1]), as_row(parts[2], last), as_row(last, last)))

        @pl.when((k < ITERS - 1) & (me < n - 1))
        def _():
            halo_copy(k + 1).start()

        return carry

    lax.fori_loop(0, ITERS, step, 0)
    squares = finalise(ITERS - 1)
    send_message(ITERS, message(as_row(squares, squares)))
    row = jnp.sqrt(total_message(ITERS)[0:1] + EPS)
    betas[ITERS - 1 : ITERS, :] = row[:, :vecs]
    inverse = wide(1.0 / as_columns(row)[:vecs])
    for j in range(blocks):
        basis[ITERS, :, block(j)] = basis[ITERS, :, block(j)] * inverse
    write_out(ITERS).start()

    for k in range(ITERS):
        @pl.when(me < n - 1)
        def _():
            halo_copy(k).wait_send()

        @pl.when(me > 0)
        def _():
            for c in range(blocks):
                back_copy(k, c).wait_send()

    for e in range(ITERS + 1):
        finish_message(e)
    for k in range(ITERS + 1):
        write_out(k).wait()


def shards(n, normals, variance, tiles, tile_ids):
    vecs, sites = normals.shape
    slots, width, _ = tiles.shape
    band = sites // width + 1
    places = band * (sites // width)
    messages = ITERS + 1
    vmem = pl.BlockSpec(memory_space=pltpu.VMEM)
    any_space = pl.BlockSpec(memory_space=pl.ANY)
    dma = pltpu.SemaphoreType.DMA
    basis, alphas, betas = pl.pallas_call(
        functools.partial(kernel, n),
        out_shape=(
            jax.ShapeDtypeStruct((ITERS + 1, vecs, sites), jnp.float32),
            jax.ShapeDtypeStruct((ITERS, vecs), jnp.float32),
            jax.ShapeDtypeStruct((ITERS, vecs), jnp.float32),
        ),
        in_specs=[pl.BlockSpec(memory_space=pltpu.SMEM), any_space, any_space, any_space],
        out_specs=(any_space, vmem, vmem),
        scratch_shapes=[
            pltpu.VMEM((vecs, sites), jnp.bfloat16),
            pltpu.VMEM((1, sites), jnp.float32),
            pltpu.VMEM((slots, width, width), jnp.bfloat16),
            pltpu.VMEM((ITERS + 1, vecs, sites), jnp.bfloat16),
            pltpu.VMEM((ITERS, vecs, sites), jnp.bfloat16),
            pltpu.VMEM((ITERS, sites // width, vecs, width), jnp.bfloat16),
            pltpu.VMEM((ITERS, sites // width, vecs, width), jnp.bfloat16),
            pltpu.VMEM((ITERS + 1, vecs, sites), jnp.float32),
            pltpu.VMEM((ITERS, vecs, sites), jnp.float32),
            pltpu.VMEM((vecs, sites), jnp.float32),
            pltpu.VMEM((ITERS + 1, vecs, LANES), jnp.float32),
            pltpu.VMEM((messages, 8, LANES), jnp.float32),
            pltpu.VMEM((messages, n, 8, LANES), jnp.float32),
            pltpu.SMEM((places,), jnp.int32),
            pltpu.SMEM((places,), jnp.float32),
            dma((slots,)),
            dma((ITERS,)),
            dma((ITERS,)),
            dma((ITERS, sites // width)),
            dma((ITERS, sites // width)),
            dma((messages,)),
            dma((messages,)),
            dma((ITERS + 1,)),
            dma((2,)),
        ],
        compiler_params=pltpu.CompilerParams(
            collective_id=0, has_side_effects=True, vmem_limit_bytes=62 * 1024 * 1024
        ),
    )(tile_ids.T, normals, variance[None, :], tiles)
    return basis * math.sqrt(sites * n), alphas, betas


def solution(mesh):
    return jax.shard_map(
        functools.partial(shards, mesh.shape["row"]),
        mesh=mesh,
        in_specs=(
            P("groups", "row"),
            P(("groups", "row")),
            P(("groups", "row"), None, None),
            P(("groups", "row"), None),
        ),
        out_specs=(P(None, "groups", "row"), P(None, "groups"), P(None, "groups")),
        check_vma=False,
    )
```

```python
import functools
import math

import jax
import jax.numpy as jnp
from jax import lax
from jax.experimental import pallas as pl
from jax.experimental.pallas import tpu as pltpu
from jax.sharding import PartitionSpec as P

ITERS = 3
EPS = 1e-06
LANES = 128


def dot(a, b, transposed):
    dims = (((1,), (1 if transposed else 0,)), ((), ()))
    return lax.dot_general(a, b, dims, preferred_element_type=jnp.float32)


def lane_sums(value):
    total = value[:, :LANES]
    for at in range(LANES, value.shape[1], LANES):
        total = total + value[:, at : at + LANES]
    return total


def as_row(first, second):
    stacked = jnp.concatenate([first, second], axis=0)
    return jnp.sum(jnp.transpose(stacked), axis=0, keepdims=True)


def as_columns(row):
    return jnp.transpose(jnp.broadcast_to(row, (LANES, LANES)))


def kernel(
    n, ids, normals, variance, tiles, basis_out, alphas, betas,
    tiles_v, vq, prev, reach_s, reach_r, basis, applied, image, coef, psend, precv, slot_map, live_map,
    tile_sem, halo_send, halo_recv, back_send, back_recv, msg_send, msg_recv, out_sem,
):
    me = lax.axis_index("row")
    slots, width, _ = tiles.shape
    vecs, sites = normals.shape
    blocks = sites // width
    band = blocks + 1

    def tile_copy(s):
        return pltpu.make_async_copy(tiles.at[s], tiles_v.at[s], tile_sem.at[s])

    for s in range(slots):
        tile_copy(s).start()

    barrier = pltpu.get_barrier_semaphore()

    def greet(o, carry):
        pl.semaphore_signal(
            barrier, inc=1, device_id={"row": lax.rem(me + o, n)}, device_id_type=pl.DeviceIdType.MESH
        )
        return carry

    lax.fori_loop(1, n, greet, 0)

    def block(at):
        return pl.ds(at * width, width)

    def wide(column):
        return jnp.concatenate([column] * (width // LANES), axis=1)

    def halo_copy(k):
        return pltpu.make_async_remote_copy(
            src_ref=vq.at[k], dst_ref=prev.at[k], send_sem=halo_send.at[k], recv_sem=halo_recv.at[k],
            device_id={"row": lax.rem(me + 1, n)}, device_id_type=pl.DeviceIdType.MESH,
        )

    def back_copy(k, c):
        return pltpu.make_async_remote_copy(
            src_ref=reach_s.at[k, c], dst_ref=reach_r.at[k, c],
            send_sem=back_send.at[k, c], recv_sem=back_recv.at[k, c],
            device_id={"row": lax.rem(me + n - 1, n)}, device_id_type=pl.DeviceIdType.MESH,
        )

    def send_message(e, message):
        psend[e] = message
        precv[e, me] = message

        def send(o, carry):
            pltpu.make_async_remote_copy(
                src_ref=psend.at[e], dst_ref=precv.at[e, me], send_sem=msg_send.at[e], recv_sem=msg_recv.at[e],
                device_id={"row": lax.rem(me + o, n)}, device_id_type=pl.DeviceIdType.MESH,
            ).start()
            return carry

        lax.fori_loop(1, n, send, 0)

    def total_message(e):
        everyone = precv.at[e, pl.ds(0, n - 1)]
        pltpu.make_async_copy(everyone, everyone, msg_recv.at[e]).wait()
        return jnp.sum(precv[e], axis=0)

    def finish_message(e):
        everyone = precv.at[e, pl.ds(0, n - 1)]
        pltpu.make_async_copy(everyone, everyone, msg_send.at[e]).wait()

    def message(*rows):
        pad = jnp.zeros((8 - len(rows), LANES), jnp.float32)
        return jnp.concatenate([*rows, pad], axis=0)

    for j in range(blocks):
        raw = normals[:, block(j)]
        vq[0, :, block(j)] = raw
        basis[0, :, block(j)] = raw.astype(jnp.float32)
    for m in range(1, ITERS):
        basis[m] = jnp.zeros(basis.shape[1:], jnp.float32)
    for m in range(ITERS):
        applied[m] = jnp.zeros(applied.shape[1:], jnp.float32)
        coef[m] = jnp.zeros(coef.shape[1:], jnp.float32)
    coef[ITERS] = jnp.ones(coef.shape[1:], jnp.float32)

    @pl.when(me == 0)
    def _():
        prev[...] = jnp.zeros_like(prev)

    @pl.when(me == n - 1)
    def _():
        reach_r[...] = jnp.zeros_like(reach_r)

    pl.semaphore_wait(barrier, n - 1)

    @pl.when(me < n - 1)
    def _():
        halo_copy(0).start()

    codes = [(ids[0, s] - me * blocks) * band + (ids[0, s] - ids[1, s]) for s in range(slots)]

    def locate(p, carry):
        slot, live = jnp.int32(0), jnp.float32(0)
        for s, code in enumerate(codes):
            slot = jnp.where(code == p, jnp.int32(s), slot)
            live = jnp.where(code == p, jnp.float32(1), live)
        slot_map[p] = slot
        live_map[p] = live
        return carry

    lax.fori_loop(0, blocks * band, locate, 0)

    def product(left, i, offset, transposed):
        p = i * band + offset
        return dot(left, tiles_v[slot_map[p]], transposed) * live_map[p]

    for s in range(slots):
        tile_copy(s).wait()

    def write_out(k):
        return pltpu.make_async_copy(basis.at[k], basis_out.at[k], out_sem.at[k])

    def finalise(k):
        sums = total_message(k)
        norm = jnp.sqrt(sums[2:3] + jnp.where(k == 0, 0.0, EPS))
        inverse = 1.0 / norm
        second = jnp.where(lax.broadcasted_iota(jnp.int32, (1, LANES), 1) >= vecs, 1, 0)
        near = sums[0:1] * inverse * jnp.where(second == k, inverse, 1.0)
        far = sums[1:2] * inverse * jnp.where(second + 2 == k, inverse, 1.0)
        low, high = as_columns(near), as_columns(far)
        columns = [low[:vecs], low[vecs : 2 * vecs], high[:vecs], as_columns(inverse)[:vecs]]
        for m, column in enumerate(columns):
            coef[m] = column
        alphas[pl.ds(k, 1), :] = jnp.where(
            k == 0, near[:, :vecs], jnp.where(k == 1, near[:, vecs : 2 * vecs], far[:, :vecs])
        )

        @pl.when(k > 0)
        def _():
            betas[pl.ds((k + ITERS - 1) % ITERS, 1), :] = norm[:, :vecs]

        proj = [wide(column) for column in columns]
        squares = jnp.zeros((vecs, LANES), jnp.float32)
        for j in range(blocks):
            vector = basis[k, :, block(j)] * proj[ITERS]
            basis[k, :, block(j)] = vector
            product_part = applied[k, :, block(j)] * proj[ITERS]
            applied[k, :, block(j)] = product_part
            lost = basis[0, :, block(j)] * proj[0]
            for m in range(1, ITERS):
                lost = lost + basis[m, :, block(j)] * proj[m]
            value = variance[:, block(j)] * vector + product_part - lost
            basis[k + 1, :, block(j)] = value
            squares = squares + lane_sums(value * value)
        write_out(k).start()
        return squares

    def step(k, carry):
        for c in range(blocks):
            total = None
            for i in range(c + 1):
                term = product(vq[k, :, block(i)], i, i + blocks - c, False)
                total = term if total is None else total + term
            reach_s[k, c] = total.astype(jnp.bfloat16)

            @pl.when(me > 0)
            def _():
                back_copy(k, c).start()

        for j in range(blocks):
            total = None
            for i in range(j, blocks):
                term = product(vq[k, :, block(i)], i, i - j, False)
                total = term if total is None else total + term
            for c in range(j + 1):
                total = total + product(vq[k, :, block(c)], j, j - c, True)
            image[:, block(j)] = total

        @pl.when(k > 0)
        def _():
            finalise(jnp.maximum(k - 1, 0))

        @pl.when(me > 0)
        def _():
            halo_copy(k).wait_recv()

        for j in range(blocks):
            total = image[:, block(j)]
            for c in range(j, blocks):
                total = total + product(prev[k, :, block(c)], j, j + blocks - c, True)
            image[:, block(j)] = total

        parts = [jnp.zeros((vecs, LANES), jnp.float32) for _ in range(ITERS + 1)]
        proj = [wide(coef[m]) for m in range(ITERS + 1)]
        for j in range(blocks):
            @pl.when(me < n - 1)
            def _():
                back_copy(k, j).wait_recv()

            value = (image[:, block(j)] + reach_r[k, j].astype(jnp.float32)) * proj[ITERS]
            for m in range(ITERS):
                value = value - applied[m, :, block(j)] * proj[m]
            applied[k, :, block(j)] = value
            vector = basis[k, :, block(j)]
            value = value + variance[:, block(j)] * vector
            vq[k + 1, :, block(j)] = value.astype(jnp.bfloat16)
            for m in range(ITERS):
                parts[m] = parts[m] + lane_sums(basis[m, :, block(j)] * value)
            parts[ITERS] = parts[ITERS] + lane_sums(vector * vector)
        @pl.when((k < ITERS - 1) & (me < n - 1))
        def _():
            halo_copy(k + 1).start()

        last = parts[ITERS]
        send_message(k, message(as_row(parts[0], parts[1]), as_row(parts[2], last), as_row(last, last)))

        return carry

    lax.fori_loop(0, ITERS, step, 0)
    squares = finalise(ITERS - 1)
    send_message(ITERS, message(as_row(squares, squares)))
    row = jnp.sqrt(total_message(ITERS)[0:1] + EPS)
    betas[ITERS - 1 : ITERS, :] = row[:, :vecs]
    inverse = wide(1.0 / as_columns(row)[:vecs])
    for j in range(blocks):
        basis[ITERS, :, block(j)] = basis[ITERS, :, block(j)] * inverse
    write_out(ITERS).start()

    for k in range(ITERS):
        @pl.when(me < n - 1)
        def _():
            halo_copy(k).wait_send()

        @pl.when(me > 0)
        def _():
            for c in range(blocks):
                back_copy(k, c).wait_send()

    for e in range(ITERS + 1):
        finish_message(e)
    for k in range(ITERS + 1):
        write_out(k).wait()


def shards(n, normals, variance, tiles, tile_ids):
    vecs, sites = normals.shape
    slots, width, _ = tiles.shape
    band = sites // width + 1
    places = band * (sites // width)
    messages = ITERS + 1
    vmem = pl.BlockSpec(memory_space=pltpu.VMEM)
    any_space = pl.BlockSpec(memory_space=pl.ANY)
    dma = pltpu.SemaphoreType.DMA
    basis, alphas, betas = pl.pallas_call(
        functools.partial(kernel, n),
        out_shape=(
            jax.ShapeDtypeStruct((ITERS + 1, vecs, sites), jnp.float32),
            jax.ShapeDtypeStruct((ITERS, vecs), jnp.float32),
            jax.ShapeDtypeStruct((ITERS, vecs), jnp.float32),
        ),
        in_specs=[pl.BlockSpec(memory_space=pltpu.SMEM), vmem, vmem, any_space],
        out_specs=(any_space, vmem, vmem),
        scratch_shapes=[
            pltpu.VMEM((slots, width, width), jnp.bfloat16),
            pltpu.VMEM((ITERS + 1, vecs, sites), jnp.bfloat16),
            pltpu.VMEM((ITERS, vecs, sites), jnp.bfloat16),
            pltpu.VMEM((ITERS, sites // width, vecs, width), jnp.bfloat16),
            pltpu.VMEM((ITERS, sites // width, vecs, width), jnp.bfloat16),
            pltpu.VMEM((ITERS + 1, vecs, sites), jnp.float32),
            pltpu.VMEM((ITERS, vecs, sites), jnp.float32),
            pltpu.VMEM((vecs, sites), jnp.float32),
            pltpu.VMEM((ITERS + 1, vecs, LANES), jnp.float32),
            pltpu.VMEM((messages, 8, LANES), jnp.float32),
            pltpu.VMEM((messages, n, 8, LANES), jnp.float32),
            pltpu.SMEM((places,), jnp.int32),
            pltpu.SMEM((places,), jnp.float32),
            dma((slots,)),
            dma((ITERS,)),
            dma((ITERS,)),
            dma((ITERS, sites // width)),
            dma((ITERS, sites // width)),
            dma((messages,)),
            dma((messages,)),
            dma((ITERS + 1,)),
        ],
        compiler_params=pltpu.CompilerParams(
            collective_id=0, has_side_effects=True, vmem_limit_bytes=48 * 1024 * 1024
        ),
    )(tile_ids.T, normals, variance[None, :], tiles)
    return basis * math.sqrt(sites * n), alphas, betas


def solution(mesh):
    return jax.shard_map(
        functools.partial(shards, mesh.shape["row"]),
        mesh=mesh,
        in_specs=(
            P("groups", "row"),
            P(("groups", "row")),
            P(("groups", "row"), None, None),
            P(("groups", "row"), None),
        ),
        out_specs=(P(None, "groups", "row"), P(None, "groups"), P(None, "groups")),
        check_vma=False,
    )
```
